32 devices in a mesh: rep: 2 (over x), col: 8 (over z, y), row: 2 (over core).
Axes of the slice: x: 2, y: 2, z: 4, core: 2. Of those that a mesh axis runs over, the one named last changes fastest.
Arguments:
- stored_base_codes: bfloat16 [4, 8192, 8192], P('rep', 'row', 'col'), parts along dimension 0, may hold values from -1 to 1
- previous_row_scale: float32 [4, 8192], P('rep', 'row'), parts along dimension 0, may hold values from 0.004 to 0.04
- output_side_factor: bfloat16 [4, 8192, 64], P('rep', ('row', 'col')), parts along dimension 0, may hold values from -0.75 to 0.75
- input_side_factor: bfloat16 [4, 64, 8192], P('rep', None, ('col', 'row')), parts along dimension 0, may hold values from -0.0625 to 0.0625
- magnitude: float32 [4, 8192], P('rep', 'row'), parts along dimension 0, may hold values from 8 to 32
Outputs:
- quantized: bfloat16 [4, 8192, 8192], P('rep', 'row', 'col'), parts along dimension 0
- new_scale: float32 [4, 8192], P('rep', 'row'), parts along dimension 0
The draws below stay inside these ranges and needn't reach their ends.
There are 2 independent parts, one for each index of `rep`. The reference program is written for one: setup_inputs(seed, part) draws one part's arguments, and reference() takes and returns one part's arrays. A program takes and returns all parts, laid end to end along the dimension named above; each array names one. Nothing has to cross between parts.
All inputs are finite; a program needn't handle non-finite values. Where the reference program divides by a largest or mean magnitude, that divisor is 1e-20 or more.
Results may differ from the reference program's by a relative error of at most 0.0044.
Values may be sent and summed in bfloat16 or wider, within the bound.
A program may use at most 192 MiB of HBM per device.

```python
import math
import jax
import jax.numpy as jnp
from jax import lax

D = 8192
R = 64
P_SIZE = 2


def block_levels(stream_key, shape, cuts, least, high):
    def one(position, blocks):
        heights = jax.random.uniform(jax.random.fold_in(jax.random.fold_in(stream_key, 6), position), (blocks,), jnp.float32, least / len(cuts), high / len(cuts))
        return jnp.repeat(jnp.exp(heights), shape[position] // blocks).reshape((-1,) + (1,) * (len(shape) - position - 1))

    loudness = one(*cuts[0])
    for cut in cuts[1:]:
        loudness = loudness * one(*cut)
    return loudness


def bell_draw(rng, extent, width, bound, shards=(), dtype=jnp.bfloat16):
    level = block_levels(rng, extent, shards, -0.22, 0.18) if shards else 1.0
    drawn = jax.random.normal(rng, extent, jnp.float32) * width * level
    return jnp.minimum(jnp.maximum(drawn, -bound), bound).astype(dtype)


def setup_inputs(seed: int = 0, part: int = 0) -> dict:
    key_of = jax.random.split(jax.random.key(seed), 6)
    part_splits = jax.random.split(jax.random.fold_in(key_of[5], part), 6)
    stored_base_codes = jnp.clip(jax.random.uniform(part_splits[0], (P_SIZE, D, D), jnp.float32, -1.0, 1.0) * block_levels(part_splits[0], (P_SIZE, D, D), ((1, 2), (2, 8)), -0.4, 0.0), -1.0, 1.0).astype(jnp.bfloat16)
    previous_row_scale = jnp.clip(jnp.exp(math.log(0.04) - 2.30258502 * jax.random.uniform(part_splits[1], (P_SIZE, D), jnp.float32) ** block_levels(part_splits[1], (P_SIZE, D), ((1, 2),), -0.2, 0.2)), 0.004, 0.04)
    output_side_factor = bell_draw(part_splits[2], (P_SIZE, D, R), R ** -0.5, 0.75, ((1, 16),))
    input_side_factor = bell_draw(part_splits[3], (P_SIZE, R, D), D ** -0.5, 0.0625, ((2, 16),))
    magnitude = jnp.clip(jnp.exp(math.log(32.0) - 1.3862944 * jax.random.uniform(part_splits[4], (P_SIZE, D), jnp.float32) ** block_levels(part_splits[4], (P_SIZE, D), ((1, 2),), -0.2, 0.2)), 8.0, 32.0)
    return dict(stored_base_codes=stored_base_codes, previous_row_scale=previous_row_scale, output_side_factor=output_side_factor, input_side_factor=input_side_factor, magnitude=magnitude)


adapter_scale_factor = 0.5
epsilon = 1e-06

def merge_one(stored_base_codes, previous_row_scale, output_side_factor, input_side_factor, magnitude):
    base_weight_rows = stored_base_codes.astype(jnp.float32) * previous_row_scale[:, None]
    adapter_update_delta = jnp.dot(output_side_factor, input_side_factor, preferred_element_type=jnp.float32)
    merged_weight_rows = base_weight_rows + adapter_scale_factor * adapter_update_delta
    squares = lax.optimization_barrier(jnp.sum(merged_weight_rows * merged_weight_rows, axis=1))
    factor = magnitude * lax.rsqrt(squares + epsilon)
    adapted = merged_weight_rows * factor[:, None]
    peak_vals = lax.optimization_barrier(jnp.max(jnp.abs(adapted), axis=1))
    quantized = (adapted / peak_vals[:, None]).astype(jnp.bfloat16)
    return (quantized, peak_vals)

def reference(stored_base_codes, previous_row_scale, output_side_factor, input_side_factor, magnitude):
    outputs = [merge_one(stored_base_codes[proj_idx], previous_row_scale[proj_idx], output_side_factor[proj_idx], input_side_factor[proj_idx], magnitude[proj_idx]) for proj_idx in range(P_SIZE)]
    quantized = jnp.stack([item[0] for item in outputs])
    new_scale = jnp.stack([item[1] for item in outputs])
    return (quantized, new_scale)
```

```python
import functools
import jax
import jax.numpy as jnp
from jax import lax
from jax.experimental import pallas as pl
from jax.experimental.pallas import tpu as pltpu
from jax.sharding import PartitionSpec as P

LANES = 128
epsilon = 1e-06
MESH = pl.DeviceIdType.MESH
resident = pltpu.VMEM
pin = pltpu.with_memory_space_constraint


def xor(a, b, size):
    total, bit = 0, 1
    while bit < size:
        total = total + ((a // bit + b // bit) % 2) * bit
        bit *= 2
    return total


def column(row):
    return jnp.transpose(jnp.broadcast_to(row, (LANES, LANES)))


def merge_kernel(
    dims, codes, prev, a, b, mag, merged, res,
    a_all, b_all, b_pad, part, parts_in, res_scr,
    code_sem, b_sem, z_send, y_send, a_recv, st_send, st_recv, bc_send, bc_recv,
):
    n, nz, ny, rows, cr, width, rank = dims
    chunks = rows // cr
    subs = cr // LANES
    kinds = 2 * subs
    me = lax.axis_index("col")
    core = lax.axis_index("row")
    z, y = me // ny, me % ny

    def source(t):
        k, q, j = t // (chunks * ny), (t // ny) % chunks, t % ny
        src = xor(z, k, nz) * ny + (y + j) % ny
        return k, q, j, src

    def code_copy(t):
        _, q, _, src = source(t)
        at = pl.ds(pl.multiple_of(src * rows + q * cr, cr), cr)
        return pltpu.make_async_copy(codes.at[:, at], merged.at[:, at], code_sem.at[t])

    tiles = n * chunks

    @pl.loop(0, tiles)
    def _(t):
        code_copy(t).start()

    barrier = pltpu.get_barrier_semaphore()
    pl.semaphore_signal(barrier, inc=1, device_id={"row": 1 - core}, device_id_type=MESH)

    @pl.loop(1, n)
    def _(t):
        pl.semaphore_signal(
            barrier, inc=1, device_id={"col": (me + t) % n}, device_id_type=MESH
        )

    packed = jnp.transpose(
        a[...].astype(jnp.float32).reshape(2 * rank, rows)
    ).astype(jnp.bfloat16)
    for q in range(chunks):
        a_all[q, me] = packed[q * cr:(q + 1) * cr]
    b_all[core] = b[...]
    pl.semaphore_wait(barrier, n)

    b_copy = pltpu.make_async_remote_copy(
        b, b_all.at[core], b_sem.at[0], b_sem.at[1],
        device_id={"row": 1 - core}, device_id_type=MESH,
    )
    b_copy.start()

    def z_copy(q, k):
        return pltpu.make_async_remote_copy(
            a_all.at[q, me], a_all.at[q, me], z_send.at[q, k], a_recv.at[q, me],
            device_id={"col": xor(z, k, nz) * ny + y}, device_id_type=MESH,
        )

    def y_copy(q, k):
        src = xor(z, k, nz) * ny + y
        return pltpu.make_async_remote_copy(
            a_all.at[q, src], a_all.at[q, src], y_send.at[q, k], a_recv.at[q, src],
            device_id={"col": z * ny + (y + 1) % ny}, device_id_type=MESH,
        )

    if ny > 1:
        for q in range(chunks):
            y_copy(q, 0).start()

    @pl.loop(1, nz)
    def _(k):
        for q in range(chunks):
            z_copy(q, k).start()

    b_copy.wait_recv()
    b_pad[...] = jnp.zeros_like(b_pad)
    cols = b.shape[2]
    for p in range(2):
        for r in range(2):
            b_pad[p, p * rank:(p + 1) * rank, r * cols:(r + 1) * cols] = b_all[r, p]

    def part_copy(q, src):
        return pltpu.make_async_remote_copy(
            part.at[q, src], parts_in.at[q, me], st_send.at[q, src], st_recv.at[q, me],
            device_id={"col": src}, device_id_type=MESH,
        )

    def arrived(ref, sem):
        pltpu.make_async_copy(ref, ref, sem).wait()

    block = 256 if width % 256 == 0 else LANES

    @pl.loop(0, tiles)
    def _(t):
        k, q, j, src = source(t)

        @pl.when(src != me)
        def _():
            arrived(a_all.at[q, src], a_recv.at[q, src])

        if ny > 1:
            @pl.when((j == 0) & (k > 0))
            def _():
                y_copy(q, k).start()

        code_copy(t).wait()
        for p in range(2):
            for s in range(subs):
                base = pl.multiple_of(src * rows + q * cr + s * LANES, LANES)
                at = pl.ds(base, LANES)
                scale = column(2.0 * prev[p:p + 1, at])
                lhs = a_all[q, src, s * LANES:(s + 1) * LANES]
                squares = jnp.zeros((LANES, LANES), jnp.float32)
                peaks = jnp.zeros((LANES, LANES), jnp.float32)
                for c in range(0, width, block):
                    delta = jnp.dot(
                        lhs, b_pad[p, :, c:c + block], preferred_element_type=jnp.float32
                    )
                    for d in range(0, block, LANES):
                        here = slice(c + d, c + d + LANES)
                        m = (
                            merged[p, at, here].astype(jnp.float32) * scale
                            + delta[:, d:d + LANES]
                        )
                        merged[p, at, here] = m.astype(jnp.bfloat16)
                        squares += m * m
                        peaks = jnp.maximum(peaks, jnp.abs(m))
                i = p * subs + s
                part[q, src, i:i + 1] = jnp.sum(squares.T, axis=0, keepdims=True)
                part[q, src, kinds + i:kinds + i + 1] = jnp.max(
                    peaks.T, axis=0, keepdims=True
                )

        @pl.when(src != me)
        def _():
            part_copy(q, src).start()

        @pl.when(src == me)
        def _():
            parts_in[q, me] = part[q, me]

    def res_copy(q, c):
        return pltpu.make_async_remote_copy(
            res_scr.at[q, me], res_scr.at[q, me], bc_send.at[q, c], bc_recv.at[q, me],
            device_id={"col": c}, device_id_type=MESH,
        )

    for q in range(chunks):
        @pl.loop(1, n)
        def _(t):
            c = (me + t) % n
            arrived(parts_in.at[q, c], st_recv.at[q, c])

        got = parts_in[q]
        squares = jnp.sum(got[:, :kinds], axis=0)
        peaks = jnp.max(got[:, kinds:], axis=0)
        for p in range(2):
            for s in range(subs):
                i = p * subs + s
                at = pl.ds(pl.multiple_of(me * rows + q * cr + s * LANES, LANES), LANES)
                factor = mag[p:p + 1, at] * lax.rsqrt(0.25 * squares[i:i + 1] + epsilon)
                peak = peaks[i:i + 1]
                res_scr[q, me, i:i + 1] = peak
                res_scr[q, me, kinds + i:kinds + i + 1] = 0.5 * peak * factor

        @pl.loop(1, n)
        def _(t):
            res_copy(q, (me + t) % n).start()

    b_copy.wait_send()
    for q in range(chunks):
        @pl.loop(1, nz)
        def _(k):
            z_copy(q, k).wait_send()

        if ny > 1:
            @pl.loop(0, nz)
            def _(k):
                y_copy(q, k).wait_send()

        @pl.loop(1, n)
        def _(t):
            c = (me + t) % n
            part_copy(q, c).wait_send()
            res_copy(q, c).wait_send()
            arrived(res_scr.at[q, c], bc_recv.at[q, c])

    res[...] = res_scr[...]


def scale_kernel(dims, slots, merged, res, out, new_scale, held, sem):
    n, nz, ny, rows, cr, width, rank = dims
    chunks = rows // cr
    subs = cr // LANES
    kinds = 2 * subs
    tiles = n * chunks

    def out_copy(t, slot):
        at = pl.ds(pl.multiple_of(t * cr, cr), cr)
        return pltpu.make_async_copy(held.at[slot], out.at[:, at], sem.at[slot])

    @pl.loop(0, tiles)
    def _(t):
        slot = t % slots
        src, q = t // chunks, t % chunks

        @pl.when(t >= slots)
        def _():
            out_copy(t - slots, slot).wait()

        for p in range(2):
            for s in range(subs):
                i = p * subs + s
                at = pl.ds(pl.multiple_of(t * cr + s * LANES, LANES), LANES)
                inverse = column(1.0 / res[q, src, i:i + 1])
                new_scale[p:p + 1, at] = res[q, src, kinds + i:kinds + i + 1]
                for c in range(0, width, LANES):
                    held[slot, p, s * LANES:(s + 1) * LANES, c:c + LANES] = (
                        merged[p, at, c:c + LANES].astype(jnp.float32) * inverse
                    ).astype(jnp.bfloat16)
        out_copy(t, slot).start()

    @pl.loop(tiles - min(slots, tiles), tiles)
    def _(t):
        out_copy(t, t % slots).wait()


def per_device(n, codes, prev, a, b, mag):
    _, out_rows, width = codes.shape
    _, rows, rank = a.shape
    cr = min(rows, 256)
    ny = 2 if n == 8 else 1
    nz = n // ny
    chunks = rows // cr
    stat = 4 * (cr // LANES)
    dims = (n, nz, ny, rows, cr, width, rank)
    vmem = pl.BlockSpec(memory_space=pltpu.VMEM)
    dma = pltpu.SemaphoreType.DMA
    merged, res = pl.pallas_call(
        functools.partial(merge_kernel, dims),
        out_shape=(
            resident(codes.shape, jnp.bfloat16),
            resident((chunks, n, stat, LANES), jnp.float32),
        ),
        in_specs=[pl.BlockSpec(memory_space=pltpu.HBM), vmem, vmem, vmem, vmem],
        out_specs=(vmem, vmem),
        scratch_shapes=[
            pltpu.VMEM((chunks, n, cr, 2 * rank), jnp.bfloat16),
            pltpu.VMEM((2,) + b.shape, jnp.bfloat16),
            pltpu.VMEM((2, 2 * rank, width), jnp.bfloat16),
            pltpu.VMEM((chunks, n, stat, LANES), jnp.float32),
            pltpu.VMEM((chunks, n, stat, LANES), jnp.float32),
            pltpu.VMEM((chunks, n, stat, LANES), jnp.float32),
            dma((n * chunks,)),
            dma((2,)),
            dma((chunks, nz)),
            dma((chunks, nz)),
            dma((chunks, n)),
            dma((chunks, n)),
            dma((chunks, n)),
            dma((chunks, n)),
            dma((chunks, n)),
        ],
        compiler_params=pltpu.CompilerParams(
            collective_id=0, has_side_effects=True, vmem_limit_bytes=16 * 2**20
        ),
        name="merge",
    )(pin(codes, pltpu.HBM), prev, jnp.swapaxes(a, 1, 2), b, mag)
    slots = 4
    return pl.pallas_call(
        functools.partial(scale_kernel, dims, slots),
        out_shape=(
            jax.ShapeDtypeStruct(codes.shape, jnp.bfloat16),
            jax.ShapeDtypeStruct(prev.shape, jnp.float32),
        ),
        in_specs=[vmem, vmem],
        out_specs=(pl.BlockSpec(memory_space=pl.ANY), vmem),
        scratch_shapes=[
            pltpu.VMEM((slots, 2, cr, width), jnp.bfloat16),
            dma((slots,)),
        ],
        compiler_params=pltpu.CompilerParams(vmem_limit_bytes=16 * 2**20),
        name="rescale",
    )(
        pin(merged, pltpu.VMEM),
        pin(res, pltpu.VMEM),
    )


def solution(mesh):
    placed = (
        P("rep", "row", "col"),
        P("rep", "row"),
        P("rep", ("row", "col"), None),
        P("rep", None, ("col", "row")),
        P("rep", "row"),
    )
    return jax.shard_map(
        functools.partial(per_device, mesh.shape["col"]),
        mesh=mesh,
        in_specs=placed,
        out_specs=(P("rep", "row", "col"), P("rep", "row")),
        check_vma=False,
    )
```

```python
import functools
import jax
import jax.numpy as jnp
from jax import lax
from jax.experimental import pallas as pl
from jax.experimental.pallas import tpu as pltpu
from jax.sharding import PartitionSpec as P

LANES = 128
epsilon = 1e-06
MESH = pl.DeviceIdType.MESH
resident = pltpu.VMEM
pin = pltpu.with_memory_space_constraint


def column(row):
    return jnp.transpose(jnp.broadcast_to(row, (LANES, LANES)))


def merge_kernel(
    dims, codes, prev_hbm, a_hbm, b_hbm, mag_hbm, merged, res,
    prev, a, b, mag, a_all, b_all, b_pad, part, parts_in, res_scr,
    in_sem, code_sem, b_sem, z_send, y_send, a_recv, st_send, st_recv, bc_send, bc_recv,
):
    n, nz, ny, rows, cr, width, rank = dims
    chunks = rows // cr
    subs = cr // LANES
    kinds = 2 * subs
    me = lax.axis_index("col")
    core = lax.axis_index("row")
    z, y = me // ny, me % ny
    beside = z * ny + (y + 1) % ny
    split = chunks - chunks // 2

    small = [
        pltpu.make_async_copy(src, dst, in_sem.at[i])
        for i, (src, dst) in enumerate(
            [(a_hbm, a), (b_hbm, b), (prev_hbm, prev), (mag_hbm, mag)]
        )
    ]
    for copy in small:
        copy.start()

    barrier = pltpu.get_barrier_semaphore()
    pl.semaphore_signal(barrier, inc=1, device_id={"row": 1 - core}, device_id_type=MESH)

    @pl.loop(1, n)
    def _(t):
        pl.semaphore_signal(
            barrier, inc=1, device_id={"col": (me + t) % n}, device_id_type=MESH
        )

    def at_place(e):
        far, down = (e + 1) // 2, (e + 1) % 2
        zs = jnp.where(down == 1, z - far, z + far)
        return far, down, zs, (zs >= 0) & (zs < nz)

    def code_copy(q, src):
        at = pl.ds(pl.multiple_of(src * rows + q * cr, cr), cr)
        return pltpu.make_async_copy(
            codes.at[:, at], merged.at[:, at], code_sem.at[q, src]
        )

    steps = (2 * nz - 1) * chunks * ny

    def place(t):
        first = ny * chunks
        late = t >= first
        u = jnp.where(late, t - first, 0)
        ring = (2 * nz - 2) * chunks
        e = jnp.where(late, 1 + (u % ring) // chunks, 0)
        j = jnp.where(late, u // ring, t // chunks)
        return e, t % chunks, j

    @pl.loop(0, steps)
    def _(t):
        e, q, j = place(t)
        _, _, zs, valid = at_place(e)

        @pl.when(valid)
        def _():
            code_copy(q, zs * ny + (y + j) % ny).start()

    small[0].wait()
    packed = jnp.transpose(
        a[...].astype(jnp.float32).reshape(2 * rank, rows)
    ).astype(jnp.bfloat16)
    for q in range(chunks):
        a_all[q, me] = packed[q * cr:(q + 1) * cr]
    small[1].wait()
    b_all[core] = b[...]
    pl.semaphore_wait(barrier, n)

    def a_copy(q, src, to, sem):
        return pltpu.make_async_remote_copy(
            a_all.at[q, src], a_all.at[q, src], sem, a_recv.at[q, src],
            device_id={"col": to}, device_id_type=MESH,
        )

    def up_copy(q, src):
        return a_copy(q, src, me + ny, z_send.at[0, q, src])

    def down_copy(q, src):
        return a_copy(q, src, me - ny, z_send.at[1, q, src])

    def y_copy(q, src):
        return a_copy(q, src, beside, y_send.at[q, src])

    b_copy = pltpu.make_async_remote_copy(
        b, b_all.at[core], b_sem.at[0], b_sem.at[1],
        device_id={"row": 1 - core}, device_id_type=MESH,
    )
    b_copy.start()

    def pass_on(e, q, j, action):
        far, down, zs, _ = at_place(e)
        src = zs * ny + (y + j) % ny
        along = (j == 0) | ((e == 0) & (q >= split))
        up = along & (z + 1 < nz) & ((e == 0) | (down == 1))
        below = along & (z > 0) & ((e == 0) | (down == 0))

        if ny > 1:
            @pl.when((j == 0) & ((far != 1) | (q < split)))
            def _():
                action(y_copy(q, src))

        @pl.when(up)
        def _():
            action(up_copy(q, src))

        @pl.when(below)
        def _():
            action(down_copy(q, src))

    for q in range(chunks):
        pass_on(0, q, 0, lambda copy: copy.start())

    small[2].wait()
    small[3].wait()
    b_copy.wait_recv()
    cols = b.shape[2]
    b_pad[...] = jnp.zeros_like(b_pad)
    for p in range(2):
        for r in range(2):
            b_pad[p, p * rank:(p + 1) * rank, r * cols:(r + 1) * cols] = b_all[r, p]

    def part_copy(src):
        return pltpu.make_async_remote_copy(
            part.at[src], parts_in.at[me], st_send.at[src], st_recv.at[me],
            device_id={"col": src}, device_id_type=MESH,
        )

    def arrived(ref, sem):
        pltpu.make_async_copy(ref, ref, sem).wait()

    block = 256 if width % 256 == 0 else LANES

    def tile(q, src):
        code_copy(q, src).wait()
        for p in range(2):
            for s in range(subs):
                base = pl.multiple_of(src * rows + q * cr + s * LANES, LANES)
                at = pl.ds(base, LANES)
                scale = column(2.0 * prev[p:p + 1, at])
                lhs = a_all[q, src, s * LANES:(s + 1) * LANES]
                squares = jnp.zeros((LANES, LANES), jnp.float32)
                peaks = jnp.zeros((LANES, LANES), jnp.float32)
                for c in range(0, width, block):
                    delta = jnp.dot(
                        lhs, b_pad[p, :, c:c + block], preferred_element_type=jnp.float32
                    )
                    for d in range(0, block, LANES):
                        here = slice(c + d, c + d + LANES)
                        m = (
                            merged[p, at, here].astype(jnp.float32) * scale
                            + delta[:, d:d + LANES]
                        )
                        merged[p, at, here] = m.astype(jnp.bfloat16)
                        squares += m * m
                        peaks = jnp.maximum(peaks, jnp.abs(m))
                i = p * subs + s
                part[src, q, i:i + 1] = jnp.sum(squares.T, axis=0, keepdims=True)
                part[src, q, kinds + i:kinds + i + 1] = jnp.max(
                    peaks.T, axis=0, keepdims=True
                )

    @pl.loop(0, steps)
    def _(t):
        e, q, j = place(t)
        _, _, zs, valid = at_place(e)
        src = zs * ny + (y + j) % ny

        @pl.when(valid)
        def _():
            @pl.when((e != 0) | (j != 0))
            def _():
                arrived(a_all.at[q, src], a_recv.at[q, src])
                pass_on(e, q, j, lambda copy: copy.start())

            tile(q, src)

            @pl.when(((e != 0) | (j != 0)) & (q == chunks - 1))
            def _():
                part_copy(src).start()

            @pl.when((e == 0) & (j == 0))
            def _():
                parts_in[src, q] = part[src, q]

    def res_copy(c):
        return pltpu.make_async_remote_copy(
            res_scr.at[me], res_scr.at[me], bc_send.at[c], bc_recv.at[me],
            device_id={"col": c}, device_id_type=MESH,
        )

    @pl.loop(1, n)
    def _(t):
        c = (me + t) % n
        arrived(parts_in.at[c], st_recv.at[c])

    for q in range(chunks):
        got = parts_in[:, q]
        squares = jnp.sum(got[:, :kinds], axis=0)
        peaks = jnp.max(got[:, kinds:], axis=0)
        for p in range(2):
            for s in range(subs):
                i = p * subs + s
                at = pl.ds(pl.multiple_of(me * rows + q * cr + s * LANES, LANES), LANES)
                factor = mag[p:p + 1, at] * lax.rsqrt(0.25 * squares[i:i + 1] + epsilon)
                peak = peaks[i:i + 1]
                res_scr[me, q, i:i + 1] = peak
                res_scr[me, q, kinds + i:kinds + i + 1] = 0.5 * peak * factor

    @pl.loop(1, n)
    def _(t):
        res_copy((me + t) % n).start()

    b_copy.wait_send()

    @pl.loop(0, steps)
    def _(t):
        e, q, j = place(t)
        _, _, _, valid = at_place(e)

        @pl.when(valid)
        def _():
            pass_on(e, q, j, lambda copy: copy.wait_send())

    @pl.loop(1, n)
    def _(t):
        c = (me + t) % n
        part_copy(c).wait_send()
        res_copy(c).wait_send()
        arrived(res_scr.at[c], bc_recv.at[c])

    res[...] = res_scr[...]


def scale_kernel(dims, slots, merged, res, out, new_scale, held, sem):
    n, nz, ny, rows, cr, width, rank = dims
    chunks = rows // cr
    subs = cr // LANES
    kinds = 2 * subs
    tiles = n * chunks

    def out_copy(t, slot):
        at = pl.ds(pl.multiple_of(t * cr, cr), cr)
        return pltpu.make_async_copy(held.at[slot], out.at[:, at], sem.at[slot])

    @pl.loop(0, tiles)
    def _(t):
        slot = t % slots
        src, q = t // chunks, t % chunks

        @pl.when(t >= slots)
        def _():
            out_copy(t - slots, slot).wait()

        for p in range(2):
            for s in range(subs):
                i = p * subs + s
                at = pl.ds(pl.multiple_of(t * cr + s * LANES, LANES), LANES)
                inverse = column(1.0 / res[src, q, i:i + 1])
                new_scale[p:p + 1, at] = res[src, q, kinds + i:kinds + i + 1]
                for c in range(0, width, LANES):
                    held[slot, p, s * LANES:(s + 1) * LANES, c:c + LANES] = (
                        merged[p, at, c:c + LANES].astype(jnp.float32) * inverse
                    ).astype(jnp.bfloat16)
        out_copy(t, slot).start()

    @pl.loop(tiles - min(slots, tiles), tiles)
    def _(t):
        out_copy(t, t % slots).wait()


def per_device(n, codes, prev, a, b, mag):
    _, out_rows, width = codes.shape
    _, rows, rank = a.shape
    cr = min(rows, 256)
    ny = 2 if n == 8 else 1
    nz = n // ny
    chunks = rows // cr
    stat = 4 * (cr // LANES)
    dims = (n, nz, ny, rows, cr, width, rank)
    vmem = pl.BlockSpec(memory_space=pltpu.VMEM)
    hbm = pl.BlockSpec(memory_space=pltpu.HBM)
    a = jnp.swapaxes(a, 1, 2)
    dma = pltpu.SemaphoreType.DMA
    merged, res = pl.pallas_call(
        functools.partial(merge_kernel, dims),
        out_shape=(
            resident(codes.shape, jnp.bfloat16),
            resident((n, chunks, stat, LANES), jnp.float32),
        ),
        in_specs=[hbm] * 5,
        out_specs=(vmem, vmem),
        scratch_shapes=[
            pltpu.VMEM(prev.shape, jnp.float32),
            pltpu.VMEM(a.shape, jnp.bfloat16),
            pltpu.VMEM(b.shape, jnp.bfloat16),
            pltpu.VMEM(mag.shape, jnp.float32),
            pltpu.VMEM((chunks, n, cr, 2 * rank), jnp.bfloat16),
            pltpu.VMEM((2,) + b.shape, jnp.bfloat16),
            pltpu.VMEM((2, 2 * rank, width), jnp.bfloat16),
            pltpu.VMEM((n, chunks, stat, LANES), jnp.float32),
            pltpu.VMEM((n, chunks, stat, LANES), jnp.float32),
            pltpu.VMEM((n, chunks, stat, LANES), jnp.float32),
            dma((4,)),
            dma((chunks, n)),
            dma((2,)),
            dma((2, chunks, n)),
            dma((chunks, n)),
            dma((chunks, n)),
            dma((n,)),
            dma((n,)),
            dma((n,)),
            dma((n,)),
        ],
        compiler_params=pltpu.CompilerParams(
            collective_id=0, has_side_effects=True, vmem_limit_bytes=16 * 2**20
        ),
        name="merge",
    )(*(pin(x, pltpu.HBM) for x in (codes, prev, a, b, mag)))
    slots = 4
    return pl.pallas_call(
        functools.partial(scale_kernel, dims, slots),
        out_shape=(
            jax.ShapeDtypeStruct(codes.shape, jnp.bfloat16),
            jax.ShapeDtypeStruct(prev.shape, jnp.float32),
        ),
        in_specs=[vmem, vmem],
        out_specs=(pl.BlockSpec(memory_space=pl.ANY), vmem),
        scratch_shapes=[
            pltpu.VMEM((slots, 2, cr, width), jnp.bfloat16),
            dma((slots,)),
        ],
        compiler_params=pltpu.CompilerParams(vmem_limit_bytes=16 * 2**20),
        name="rescale",
    )(
        pin(merged, pltpu.VMEM),
        pin(res, pltpu.VMEM),
    )


def solution(mesh):
    placed = (
        P("rep", "row", "col"),
        P("rep", "row"),
        P("rep", ("row", "col"), None),
        P("rep", None, ("col", "row")),
        P("rep", "row"),
    )
    return jax.shard_map(
        functools.partial(per_device, mesh.shape["col"]),
        mesh=mesh,
        in_specs=placed,
        out_specs=(P("rep", "row", "col"), P("rep", "row")),
        check_vma=False,
    )
```
